32 devices in a mesh: rows: 16 (over z, y, x), cols: 2 (over core).
Axes of the slice: x: 2, y: 2, z: 4, core: 2. Of those that a mesh axis runs over, the one named last changes fastest.
Arguments:
- features: float32 [16, 2048], P(None, ('rows', 'cols')), may hold values from -4 to 4
- targets: float32 [32, 2048], P(None, ('rows', 'cols')), may hold values from -6 to 6
- point_order: int32 [2048], P(('rows', 'cols')), may hold values from 0 to 2047, as said below
- lengthscale: float32 [16], replicated, may hold values from 1 to 1.8
- noise_var: float32 [32], replicated, may hold values from 0.1 to 1
Outputs:
- solution: float32 [32, 2048], P(None, ('rows', 'cols'))
- residual: float32 [32, 2048], P(None, ('rows', 'cols'))
The draws below stay inside these ranges and needn't reach their ends.
Inputs may be any that keep to these rules, and one draw needn't show every extreme that they name: `point_order`: each aligned block of 128 entries, the k-th one, holds each of the numbers k * 128 to k * 128 + 127 exactly once.
All inputs are finite; a program needn't handle non-finite values.
Results may differ from the reference program's by a relative error of at most 0.0051.
Values may be sent and summed in bfloat16 or wider, within the bound.
A program may use at most 64 MiB of HBM per device.

```python
import math
import jax
import jax.numpy as jnp
from jax import lax

FEATS = 16
RHS = 32
INNER = 3
OUTER = 2
BLOCK = 128
POINTS = 2048
N_ROWS = 16


def draw_point_order(key, part):
    blocks = POINTS // BLOCK
    keys = jax.random.split(jax.random.fold_in(key, 7), blocks)
    shuffled = jax.vmap(lambda subkey: jax.random.permutation(subkey, BLOCK))(keys)
    offsets = jnp.arange(blocks, dtype=jnp.int32) * BLOCK
    return (shuffled.astype(jnp.int32) + offsets[:, None]).reshape(POINTS)


def draw_features(key, part):
    subkey = jax.random.fold_in(key, 11)
    return jnp.clip(jax.random.normal(subkey, (FEATS, POINTS), jnp.float32), -4.0, 4.0)


def steps_of(rng, extent, cuts, least, high):
    factor_of, own = 1.0, jax.random.fold_in(rng, 6)
    for position, shards_of in cuts:
        steps = jnp.exp(jax.random.uniform(jax.random.fold_in(own, position), (shards_of,), jnp.float32, least / len(cuts), high / len(cuts)))
        factor_of = factor_of * jnp.repeat(steps, extent[position] // shards_of).reshape([-1 if axis == position else 1 for axis in range(len(extent))])
    return factor_of


def scatter_about(key, extent, scale, limit, cuts=(), kind=jnp.bfloat16):
    factor_of = steps_of(key, extent, cuts, -0.22, 0.18) if cuts else 1.0
    array = jax.random.normal(key, extent, jnp.float32) * scale * factor_of
    return jnp.minimum(jnp.maximum(array, -limit), limit).astype(kind)


def setup_inputs(seed: int = 0) -> dict:
    seeds = jax.random.split(jax.random.key(seed), 6)
    features = draw_features(jax.random.fold_in(seeds[5], 71), 0)
    targets = scatter_about(seeds[1], (RHS, POINTS), 1.0, 6.0, ((1, 32),), jnp.float32)
    point_order = draw_point_order(jax.random.fold_in(seeds[5], 71), 0)
    lengthscale = jnp.clip(jnp.exp(jax.random.uniform(seeds[3], (FEATS,), jnp.float32, math.log(1.0), math.log(1.8))), 1.0, 1.8)
    noise_var = jnp.clip(jnp.exp(jax.random.uniform(seeds[4], (RHS,), jnp.float32, math.log(0.1), math.log(1.0))), 0.1, 1.0)
    return dict(features=features, targets=targets, point_order=point_order, lengthscale=lengthscale, noise_var=noise_var)


def kernel_tile(col_feat, col_norm, row_feat, row_norm):
    inner_prod = jnp.dot(col_feat.T, row_feat, precision=lax.Precision.HIGHEST, preferred_element_type=jnp.float32)
    return jnp.exp(-0.5 * (col_norm[:, None] + row_norm[None, :] - 2.0 * inner_prod)).astype(jnp.bfloat16)


def apply_full(vectors, scaled, norms, noise_var):
    packed = lax.optimization_barrier(vectors.astype(jnp.bfloat16)).astype(jnp.float32)
    points = scaled.shape[1]
    span_rows = math.gcd(points, 512)

    def one_block(which):
        row_feat = lax.dynamic_slice_in_dim(scaled, which * span_rows, span_rows, 1)
        row_norm = lax.dynamic_slice_in_dim(norms, which * span_rows, span_rows, 0)
        kern_tile = lax.optimization_barrier(kernel_tile(scaled, norms, row_feat, row_norm)).astype(jnp.float32)
        return jnp.dot(packed, kern_tile, precision=lax.Precision.HIGHEST, preferred_element_type=jnp.float32)

    result = lax.map(one_block, jnp.arange(points // span_rows, dtype=jnp.int32))
    result = jnp.transpose(result, (1, 0, 2)).reshape(vectors.shape)
    return result + noise_var[:, None] * vectors


def block_kernels(scaled, norms):
    blocked = scaled.reshape(FEATS, N_ROWS, BLOCK).transpose(1, 0, 2)
    block_norms = norms.reshape(N_ROWS, BLOCK)

    def single(pair):
        return kernel_tile(pair[0], pair[1], pair[0], pair[1])

    return lax.map(single, (blocked, block_norms))


def block_solve(residual, kernels, noise_var):
    kern_wide = kernels.astype(jnp.float32)
    rhs_blocks = residual.reshape(RHS, N_ROWS, BLOCK)
    res_norm = jnp.sum(rhs_blocks * rhs_blocks, 2)
    direction = rhs_blocks
    correction = jnp.zeros_like(rhs_blocks)
    for inner_turn in range(INNER):
        packed = lax.optimization_barrier(direction.astype(jnp.bfloat16)).astype(jnp.float32)
        applied = jnp.einsum("rbj,bji->rbi", packed, kern_wide, precision=lax.Precision.HIGHEST)
        applied = applied + noise_var[:, None, None] * direction
        curvature = jnp.sum(direction * applied, 2)
        step_len = res_norm / curvature
        correction = correction + step_len[:, :, None] * direction
        rhs_blocks = rhs_blocks - step_len[:, :, None] * applied
        if inner_turn + 1 < INNER:
            new_norm = jnp.sum(rhs_blocks * rhs_blocks, 2)
            direction = rhs_blocks + (new_norm / res_norm)[:, :, None] * direction
            res_norm = new_norm
    return correction.reshape(RHS, N_ROWS * BLOCK)


def reference(features, targets, point_order, lengthscale, noise_var):
    scaled = features / lengthscale[:, None]
    norms = jnp.sum(scaled * scaled, 0)
    residual = jnp.take(targets, point_order, axis=1)
    kernels = block_kernels(scaled, norms)
    solution = jnp.zeros_like(residual)
    for outer_turn in range(OUTER):
        correction = block_solve(residual, kernels, noise_var)
        applied = apply_full(correction, scaled, norms, noise_var)
        cross_term = jnp.sum(residual * applied, 1)
        energy = jnp.sum(applied * applied, 1)
        damping_w = cross_term / (energy + 1e-6)
        solution = solution + damping_w[:, None] * correction
        residual = residual - damping_w[:, None] * applied
    return solution, residual
```

```python
import functools
import math

import jax
import jax.numpy as jnp
from jax import lax
from jax.experimental import pallas as pl
from jax.experimental.pallas import tpu as pltpu
from jax.sharding import PartitionSpec as P

INNER = 3
OUTER = 2
MESH = pl.DeviceIdType.MESH
HIGH = lax.Precision.HIGHEST


def kernel_tile(col_feat, col_norm, row_feat, row_norm):
    inner_prod = jnp.dot(
        col_feat.T, row_feat, precision=lax.Precision.HIGHEST, preferred_element_type=jnp.float32
    )
    return jnp.exp(-0.5 * (col_norm[:, None] + row_norm[None, :] - 2.0 * inner_prod)).astype(
        jnp.bfloat16
    )


def apply_columns(running, portion, col_feat, col_norm, row_feat, row_norm):
    columns = portion.shape[1]
    sub_cols = math.gcd(columns, 512)

    def advance(which, summed):
        offset = which * sub_cols
        part_feat = lax.dynamic_slice_in_dim(col_feat, offset, sub_cols, 1)
        part_norm = lax.dynamic_slice_in_dim(col_norm, offset, sub_cols, 0)
        part_vec = lax.dynamic_slice_in_dim(portion, offset, sub_cols, 1)
        kern_tile = kernel_tile(part_feat, part_norm, row_feat, row_norm)
        return summed + jnp.dot(part_vec, kern_tile, preferred_element_type=jnp.float32)

    return lax.fori_loop(0, columns // sub_cols, advance, running)


def body_large(features, targets, point_order, lengthscale, noise_var):
    scaled = features / lengthscale[:, None]
    row_norms = jnp.sum(scaled * scaled, 0)
    block_feat, block_targ = (
        lax.all_gather(scaled, "cols", axis=1, tiled=True),
        lax.all_gather(targets, "cols", axis=1, tiled=True),
    )
    block_norms = jnp.sum(block_feat * block_feat, 0)
    block_first = lax.axis_index("rows") * block_feat.shape[1]
    residual = jnp.take(block_targ, point_order - block_first, axis=1)
    noise_col = noise_var[:, None]
    own_len = scaled.shape[1]
    col_feat = lax.all_gather(scaled, ("rows", "cols"), axis=1, tiled=True)
    col_norm = jnp.sum(col_feat * col_feat, 0)
    solution = jnp.zeros_like(residual)
    for outer_turn in range(OUTER):
        remains = lax.all_gather(residual, "cols", axis=1, tiled=True)
        res_norm = jnp.sum(remains * remains, 1)
        direction = remains
        correction = jnp.zeros_like(remains)
        for inner_turn in range(INNER):
            block_packed = direction.astype(jnp.bfloat16)
            blank_block = jnp.zeros(block_packed.shape, jnp.float32)
            applied = (
                apply_columns(
                    blank_block, block_packed, block_feat, block_norms, block_feat, block_norms
                )
                + noise_col * direction
            )
            curvature = jnp.sum(direction * applied, 1)
            step_len = res_norm / curvature
            correction = correction + step_len[:, None] * direction
            remains = remains - step_len[:, None] * applied
            if inner_turn + 1 < INNER:
                new_norm = jnp.sum(remains * remains, 1)
                direction = remains + (new_norm / res_norm)[:, None] * direction
                res_norm = new_norm
        correction = lax.dynamic_slice_in_dim(
            correction, lax.axis_index("cols") * own_len, own_len, 1
        )
        packed = correction.astype(jnp.bfloat16)
        blank = jnp.zeros((packed.shape[0], scaled.shape[1]), jnp.float32)
        applied = (
            apply_columns(
                blank,
                lax.all_gather(packed, ("rows", "cols"), axis=1, tiled=True),
                col_feat,
                col_norm,
                scaled,
                row_norms,
            )
            + noise_col * correction
        )
        cross_term, energy = lax.psum(
            (jnp.sum(residual * applied, 1), jnp.sum(applied * applied, 1)), ("rows", "cols")
        )
        damping_w = cross_term / (energy + 1e-06)
        solution = solution + damping_w[:, None] * correction
        residual = residual - damping_w[:, None] * applied
    return (solution, residual)


def to_column(row, rhs):
    shape = (rhs, row.shape[1])
    on_diag = lax.broadcasted_iota(jnp.int32, shape, 0) == lax.broadcasted_iota(jnp.int32, shape, 1)
    return jnp.sum(jnp.where(on_diag, row, 0.0), 1, keepdims=True)


def to_row(column, lanes):
    shape = (column.shape[0], lanes)
    on_diag = lax.broadcasted_iota(jnp.int32, shape, 0) == lax.broadcasted_iota(jnp.int32, shape, 1)
    return jnp.sum(jnp.where(on_diag, column, 0.0), 0, keepdims=True)


def fused(
    n_rows,
    n_cols,
    feat_ref,
    targ_ref,
    order_ref,
    length_ref,
    noise_ref,
    sol_ref,
    res_ref,
    parts,
    feats,
    tiles,
    corrs,
    sums,
    part_send,
    part_recv,
    feat_send,
    feat_recv,
    corr_send,
    corr_recv,
    sum_send,
    sum_recv,
):
    row, col = lax.axis_index("rows"), lax.axis_index("cols")
    n_feats, own_len = feat_ref.shape
    rhs = targ_ref.shape[0]
    block = n_cols * own_len

    def row_peer(k):
        return lax.rem(row + k, n_rows)

    def col_peer(k):
        return lax.rem(col + k, n_cols)

    def each(count, step):
        def one(k, carry):
            step(k)
            return carry

        lax.fori_loop(1, count, one, 0)

    barrier = pltpu.get_barrier_semaphore()
    each(
        n_cols,
        lambda k: pl.semaphore_signal(
            barrier, inc=1, device_id=(row, col_peer(k)), device_id_type=MESH
        ),
    )
    each(
        n_rows,
        lambda k: pl.semaphore_signal(
            barrier, inc=1, device_id=(row_peer(k), col), device_id_type=MESH
        ),
    )

    noise_col = to_column(noise_ref[...], rhs)
    scaled = feat_ref[...] / to_column(length_ref[...], n_feats)
    order = (order_ref[...] - row * block).astype(jnp.float32)
    own = jnp.concatenate(
        [scaled, targ_ref[...], jnp.broadcast_to(order, (8, own_len))], axis=0
    )
    wide = jnp.concatenate([own] * n_cols, axis=1)
    lane = lax.broadcasted_iota(jnp.int32, wide.shape, 1)
    parts[col] = jnp.where(lane // own_len == col, wide, 0.0)
    pl.semaphore_wait(barrier, n_rows - 1 + n_cols - 1)

    def part_copy(k, slot):
        return pltpu.make_async_remote_copy(
            src_ref=parts.at[slot],
            dst_ref=parts.at[slot],
            send_sem=part_send.at[k],
            recv_sem=part_recv.at[k],
            device_id=(row, col_peer(k)),
            device_id_type=MESH,
        )

    each(n_cols, lambda k: part_copy(k, col).start())
    each(n_cols, lambda k: part_copy(k, col_peer(n_cols - k)).wait_recv())
    whole = parts[0]
    for c in range(1, n_cols):
        whole = whole + parts[c]
    block_feat = whole[:n_feats]
    block_targ = whole[n_feats : n_feats + rhs]
    block_order = whole[n_feats + rhs : n_feats + rhs + 1]
    feats[row] = block_feat

    def feat_copy(k, slot):
        return pltpu.make_async_remote_copy(
            src_ref=feats.at[slot],
            dst_ref=feats.at[slot],
            send_sem=feat_send.at[k],
            recv_sem=feat_recv.at[k],
            device_id=(row_peer(k), col),
            device_id_type=MESH,
        )

    each(n_rows, lambda k: feat_copy(k, row).start())

    place = lax.broadcasted_iota(jnp.int32, (block, block), 0).astype(jnp.float32)
    picked = jnp.where(place == block_order, 1.0, 0.0)
    residual = jnp.dot(block_targ, picked, precision=HIGH, preferred_element_type=jnp.float32)

    own_feat = jnp.transpose(block_feat)
    own_norm = jnp.sum(own_feat * own_feat, 1, keepdims=True)

    def tile_of(feat):
        norm = jnp.sum(feat * feat, 0, keepdims=True)
        inner_prod = jnp.dot(own_feat, feat, precision=HIGH, preferred_element_type=jnp.float32)
        return jnp.exp(-0.5 * (own_norm + norm - 2.0 * inner_prod)).astype(jnp.bfloat16)

    block_tile = tile_of(block_feat)

    def solve(residual):
        remains = residual
        res_norm = jnp.sum(remains * remains, 1, keepdims=True)
        direction = remains
        correction = jnp.zeros_like(remains)
        for inner_turn in range(INNER):
            image = (
                jnp.dot(
                    direction.astype(jnp.bfloat16), block_tile, preferred_element_type=jnp.float32
                )
                + noise_col * direction
            )
            step_len = res_norm / jnp.sum(direction * image, 1, keepdims=True)
            correction = correction + step_len * direction
            if inner_turn + 1 < INNER:
                remains = remains - step_len * image
                new_norm = jnp.sum(remains * remains, 1, keepdims=True)
                direction = remains + (new_norm / res_norm) * direction
                res_norm = new_norm
        return correction

    def corr_copy(turn, k, slot):
        return pltpu.make_async_remote_copy(
            src_ref=corrs.at[turn, slot],
            dst_ref=corrs.at[turn, slot],
            send_sem=corr_send.at[turn, k],
            recv_sem=corr_recv.at[turn, k],
            device_id=(row_peer(k), col),
            device_id_type=MESH,
        )

    def sum_copy(turn, k, slot):
        return pltpu.make_async_remote_copy(
            src_ref=sums.at[turn, slot],
            dst_ref=sums.at[turn, slot],
            send_sem=sum_send.at[turn, k],
            recv_sem=sum_recv.at[turn, k],
            device_id=(row_peer(k), col),
            device_id_type=MESH,
        )

    solved = jnp.zeros_like(residual)
    for turn in range(OUTER):
        correction = solve(residual)
        corrs[turn, row] = correction.astype(jnp.bfloat16)
        each(n_rows, lambda k: corr_copy(turn, k, row).start())
        if turn == 0:
            each(n_rows, lambda k: feat_copy(k, row_peer(n_rows - k)).wait_recv())
            for b in range(n_rows):
                tiles[b] = tile_of(feats[b])
        each(n_rows, lambda k: corr_copy(turn, k, row_peer(n_rows - k)).wait_recv())
        applied = noise_col * correction
        for b in range(n_rows):
            applied = applied + lax.dot_general(
                corrs[turn, b],
                tiles[b],
                (((1,), (1,)), ((), ())),
                preferred_element_type=jnp.float32,
            )
        lanes = sums.shape[-1]
        cross = to_row(jnp.sum(residual * applied, 1, keepdims=True), lanes)
        energy = to_row(jnp.sum(applied * applied, 1, keepdims=True), lanes)
        sums[turn, row] = jnp.concatenate([cross, energy], axis=0)
        each(n_rows, lambda k: sum_copy(turn, k, row).start())
        each(n_rows, lambda k: sum_copy(turn, k, row_peer(n_rows - k)).wait_recv())
        total = jnp.sum(sums[turn], 0)
        damping = to_column(total[0:1] / (total[1:2] + 1e-06), rhs)
        solved = solved + damping * correction
        residual = residual - damping * applied

    def own_part(field):
        picked_part = field[:, :own_len]
        for c in range(1, n_cols):
            picked_part = jnp.where(
                col == c, field[:, c * own_len : (c + 1) * own_len], picked_part
            )
        return picked_part

    sol_ref[...] = own_part(solved)
    res_ref[...] = own_part(residual)
    each(n_cols, lambda k: part_copy(k, col).wait_send())
    each(n_rows, lambda k: feat_copy(k, row).wait_send())
    for turn in range(OUTER):
        each(n_rows, lambda k: corr_copy(turn, k, row).wait_send())
        each(n_rows, lambda k: sum_copy(turn, k, row).wait_send())


def body_small(n_rows, n_cols, features, targets, point_order, lengthscale, noise_var):
    n_feats, own_len = features.shape
    rhs = targets.shape[0]
    block = n_cols * own_len
    out = jax.ShapeDtypeStruct((rhs, own_len), jnp.float32)
    vmem = pl.BlockSpec(memory_space=pltpu.VMEM)
    dma = pltpu.SemaphoreType.DMA
    return pl.pallas_call(
        functools.partial(fused, n_rows, n_cols),
        out_shape=(out, out),
        in_specs=[vmem] * 5,
        out_specs=(vmem, vmem),
        scratch_shapes=[
            pltpu.VMEM((n_cols, n_feats + rhs + 8, block), jnp.float32),
            pltpu.VMEM((n_rows, n_feats, block), jnp.float32),
            pltpu.VMEM((n_rows, block, block), jnp.bfloat16),
            pltpu.VMEM((OUTER, n_rows, rhs, block), jnp.bfloat16),
            pltpu.VMEM((OUTER, n_rows, 2, 128), jnp.float32),
            dma((n_cols,)),
            dma((n_cols,)),
            dma((n_rows,)),
            dma((n_rows,)),
            dma((OUTER, n_rows)),
            dma((OUTER, n_rows)),
            dma((OUTER, n_rows)),
            dma((OUTER, n_rows)),
        ],
        compiler_params=pltpu.CompilerParams(
            collective_id=0, has_side_effects=True, vmem_limit_bytes=32 * 1024 * 1024
        ),
    )(features, targets, point_order[None, :], lengthscale[None, :], noise_var[None, :])


def body(n_rows, n_cols, features, targets, point_order, lengthscale, noise_var):
    n_feats, own_len = features.shape
    rhs = targets.shape[0]
    block = n_cols * own_len
    args = (features, targets, point_order, lengthscale, noise_var)
    fits = 2 * n_rows * block * block <= 8 * 1024 * 1024
    even = block % 128 == 0 and rhs % 16 == 0 and rhs <= 128 and n_feats % 8 == 0
    if fits and even and n_rows > 1 and n_cols > 1:
        return body_small(n_rows, n_cols, *args)
    return body_large(*args)


def solution(mesh):
    return jax.shard_map(
        functools.partial(body, mesh.shape["rows"], mesh.shape["cols"]),
        mesh=mesh,
        in_specs=(
            P(None, ("rows", "cols")),
            P(None, ("rows", "cols")),
            P(("rows", "cols")),
            P(),
            P(),
        ),
        out_specs=(P(None, ("rows", "cols")), P(None, ("rows", "cols"))),
        check_vma=False,
    )
```

```python
import functools
import math

import jax
import jax.numpy as jnp
from jax import lax
from jax.experimental import pallas as pl
from jax.experimental.pallas import tpu as pltpu
from jax.sharding import PartitionSpec as P

INNER = 3
OUTER = 2
MESH = pl.DeviceIdType.MESH


def kernel_tile(col_feat, col_norm, row_feat, row_norm):
    inner_prod = jnp.dot(
        col_feat.T, row_feat, precision=lax.Precision.HIGHEST, preferred_element_type=jnp.float32
    )
    return jnp.exp(-0.5 * (col_norm[:, None] + row_norm[None, :] - 2.0 * inner_prod)).astype(
        jnp.bfloat16
    )


def apply_columns(running, portion, col_feat, col_norm, row_feat, row_norm):
    columns = portion.shape[1]
    sub_cols = math.gcd(columns, 512)

    def advance(which, summed):
        offset = which * sub_cols
        part_feat = lax.dynamic_slice_in_dim(col_feat, offset, sub_cols, 1)
        part_norm = lax.dynamic_slice_in_dim(col_norm, offset, sub_cols, 0)
        part_vec = lax.dynamic_slice_in_dim(portion, offset, sub_cols, 1)
        kern_tile = kernel_tile(part_feat, part_norm, row_feat, row_norm)
        return summed + jnp.dot(part_vec, kern_tile, preferred_element_type=jnp.float32)

    return lax.fori_loop(0, columns // sub_cols, advance, running)


def body_large(features, targets, point_order, lengthscale, noise_var):
    scaled = features / lengthscale[:, None]
    row_norms = jnp.sum(scaled * scaled, 0)
    block_feat, block_targ = (
        lax.all_gather(scaled, "cols", axis=1, tiled=True),
        lax.all_gather(targets, "cols", axis=1, tiled=True),
    )
    block_norms = jnp.sum(block_feat * block_feat, 0)
    block_first = lax.axis_index("rows") * block_feat.shape[1]
    residual = jnp.take(block_targ, point_order - block_first, axis=1)
    noise_col = noise_var[:, None]
    own_len = scaled.shape[1]
    col_feat = lax.all_gather(scaled, ("rows", "cols"), axis=1, tiled=True)
    col_norm = jnp.sum(col_feat * col_feat, 0)
    solution = jnp.zeros_like(residual)
    for outer_turn in range(OUTER):
        remains = lax.all_gather(residual, "cols", axis=1, tiled=True)
        res_norm = jnp.sum(remains * remains, 1)
        direction = remains
        correction = jnp.zeros_like(remains)
        for inner_turn in range(INNER):
            block_packed = direction.astype(jnp.bfloat16)
            blank_block = jnp.zeros(block_packed.shape, jnp.float32)
            applied = (
                apply_columns(
                    blank_block, block_packed, block_feat, block_norms, block_feat, block_norms
                )
                + noise_col * direction
            )
            curvature = jnp.sum(direction * applied, 1)
            step_len = res_norm / curvature
            correction = correction + step_len[:, None] * direction
            remains = remains - step_len[:, None] * applied
            if inner_turn + 1 < INNER:
                new_norm = jnp.sum(remains * remains, 1)
                direction = remains + (new_norm / res_norm)[:, None] * direction
                res_norm = new_norm
        correction = lax.dynamic_slice_in_dim(
            correction, lax.axis_index("cols") * own_len, own_len, 1
        )
        packed = correction.astype(jnp.bfloat16)
        blank = jnp.zeros((packed.shape[0], scaled.shape[1]), jnp.float32)
        applied = (
            apply_columns(
                blank,
                lax.all_gather(packed, ("rows", "cols"), axis=1, tiled=True),
                col_feat,
                col_norm,
                scaled,
                row_norms,
            )
            + noise_col * correction
        )
        cross_term, energy = lax.psum(
            (jnp.sum(residual * applied, 1), jnp.sum(applied * applied, 1)), ("rows", "cols")
        )
        damping_w = cross_term / (energy + 1e-06)
        solution = solution + damping_w[:, None] * correction
        residual = residual - damping_w[:, None] * applied
    return (solution, residual)


def to_column(row, rows, first=0):
    shape = (rows, row.shape[1])
    at, lane = (lax.broadcasted_iota(jnp.int32, shape, axis) for axis in (0, 1))
    return jnp.sum(jnp.where(at + first == lane, row, 0.0), 1, keepdims=True)


def to_row(columns, lanes):
    rows = columns[0].shape[0]
    at, lane = (lax.broadcasted_iota(jnp.int32, (rows, lanes), axis) for axis in (0, 1))
    placed = jnp.zeros((rows, lanes), jnp.float32)
    for which, column in enumerate(columns):
        placed = jnp.where(at + which * rows == lane, column, placed)
    return jnp.sum(placed, 0, keepdims=True)


def three_parts(x):
    high = x.astype(jnp.bfloat16).astype(jnp.float32)
    mid = (x - high).astype(jnp.bfloat16).astype(jnp.float32)
    low = ((x - high) - mid).astype(jnp.bfloat16).astype(jnp.float32)
    return high, mid, low


def fused(
    n_rows,
    n_cols,
    feat_hbm,
    targ_hbm,
    order_hbm,
    length_hbm,
    noise_hbm,
    sol_ref,
    res_ref,
    feat_ref,
    targ_ref,
    order_ref,
    length_ref,
    noise_ref,
    parts_out,
    parts,
    feats,
    tiles,
    corrs,
    sums,
    ends,
    load_sem,
    part_send,
    part_recv,
    feat_send,
    feat_recv,
    corr_send,
    corr_recv,
    sum_send,
    sum_recv,
    end_send,
    end_recv,
):
    row, col = lax.axis_index("rows"), lax.axis_index("cols")
    n_feats, own_len = feat_ref.shape
    own_rhs = targ_ref.shape[0] // n_cols
    block = n_cols * own_len

    def row_peer(k):
        return lax.rem(row + k, n_rows)

    def col_peer(k):
        return lax.rem(col + k, n_cols)

    def each(count, step):
        def one(k, carry):
            step(k)
            return carry

        lax.fori_loop(1, count, one, 0)

    loads = [
        pltpu.make_async_copy(source, target, load_sem.at[which])
        for which, (source, target) in enumerate(
            (
                (feat_hbm, feat_ref),
                (targ_hbm, targ_ref),
                (order_hbm, order_ref),
                (length_hbm, length_ref),
                (noise_hbm, noise_ref),
            )
        )
    ]
    for load in loads:
        load.start()

    barrier = pltpu.get_barrier_semaphore()
    each(
        n_cols,
        lambda k: pl.semaphore_signal(
            barrier, inc=1, device_id=(row, col_peer(k)), device_id_type=MESH
        ),
    )
    each(
        n_rows,
        lambda k: pl.semaphore_signal(
            barrier, inc=1, device_id=(row_peer(k), col), device_id_type=MESH
        ),
    )
    for load in loads:
        load.wait()

    noise_col = to_column(noise_ref[...], own_rhs, col * own_rhs)
    scaled = feat_ref[...] / to_column(length_ref[...], n_feats)
    order = (order_ref[...] - row * block).astype(jnp.float32)
    order = jnp.broadcast_to(order, (8, own_len))
    for c in range(n_cols):
        share = targ_ref[c * own_rhs : (c + 1) * own_rhs, :]
        own = jnp.concatenate([scaled, share, order], axis=0)
        wide = jnp.concatenate([own] * n_cols, axis=1)
        lane = lax.broadcasted_iota(jnp.int32, wide.shape, 1)
        parts_out[c] = jnp.where(lane // own_len == col, wide, 0.0)
    pl.semaphore_wait(barrier, n_rows - 1 + n_cols - 1)

    def part_copy(k, target, slot):
        return pltpu.make_async_remote_copy(
            src_ref=parts_out.at[target],
            dst_ref=parts.at[slot],
            send_sem=part_send.at[k],
            recv_sem=part_recv.at[k],
            device_id=(row, target),
            device_id_type=MESH,
        )

    each(n_cols, lambda k: part_copy(k, col_peer(k), col).start())
    parts[col] = parts_out[col]
    each(n_cols, lambda k: part_copy(k, col_peer(k), col_peer(n_cols - k)).wait_recv())
    whole = parts[0]
    for c in range(1, n_cols):
        whole = whole + parts[c]
    block_feat = whole[:n_feats]
    block_targ = whole[n_feats : n_feats + own_rhs]
    block_order = whole[n_feats + own_rhs : n_feats + own_rhs + 1]
    feats[row] = block_feat

    def row_copy(buffer, send_sem, recv_sem, k, slot):
        return pltpu.make_async_remote_copy(
            src_ref=buffer.at[slot],
            dst_ref=buffer.at[slot],
            send_sem=send_sem.at[k],
            recv_sem=recv_sem.at[k],
            device_id=(row_peer(k), col),
            device_id_type=MESH,
        )

    def spread(*copy):
        each(n_rows, lambda k: row_copy(*copy, k, row).start())

    def arrive(*copy):
        each(n_rows, lambda k: row_copy(*copy, k, row_peer(n_rows - k)).wait_recv())

    feat_args = (feats, feat_send, feat_recv)
    corr_args = [(corrs.at[t], corr_send.at[t], corr_recv.at[t]) for t in range(OUTER)]
    sum_args = [(sums.at[t], sum_send.at[t], sum_recv.at[t]) for t in range(OUTER)]

    spread(*feat_args)

    place = lax.broadcasted_iota(jnp.int32, (block, block), 0).astype(jnp.float32)
    picked = jnp.where(place == block_order, 1.0, 0.0).astype(jnp.bfloat16)
    three = jnp.concatenate(three_parts(block_targ), axis=0).astype(jnp.bfloat16)
    three = jnp.dot(three, picked, preferred_element_type=jnp.float32)
    residual = (three[:own_rhs] + three[own_rhs : 2 * own_rhs]) + three[2 * own_rhs :]

    high, mid, low = three_parts(block_feat)
    own_stack = jnp.transpose(jnp.concatenate([high, high, mid, mid, high, low], axis=0))
    own_stack = own_stack.astype(jnp.bfloat16)
    own_norm = jnp.transpose(
        jnp.broadcast_to(jnp.sum(block_feat * block_feat, 0, keepdims=True), (8, block))
    )[:, :1]

    def tile_of(feat):
        norm = jnp.sum(feat * feat, 0, keepdims=True)
        high, mid, low = three_parts(feat)
        stack = jnp.concatenate([high, mid, high, mid, low, high], axis=0).astype(jnp.bfloat16)
        inner_prod = jnp.dot(own_stack, stack, preferred_element_type=jnp.float32)
        return jnp.exp(-0.5 * (own_norm + norm - 2.0 * inner_prod)).astype(jnp.bfloat16)

    block_tile = tile_of(block_feat)

    def solve(residual):
        remains = residual
        res_norm = jnp.sum(remains * remains, 1, keepdims=True)
        direction = remains
        correction = jnp.zeros_like(remains)
        for inner_turn in range(INNER):
            image = (
                jnp.dot(
                    direction.astype(jnp.bfloat16), block_tile, preferred_element_type=jnp.float32
                )
                + noise_col * direction
            )
            step_len = res_norm / jnp.sum(direction * image, 1, keepdims=True)
            correction = correction + step_len * direction
            if inner_turn + 1 < INNER:
                remains = remains - step_len * image
                new_norm = jnp.sum(remains * remains, 1, keepdims=True)
                direction = remains + (new_norm / res_norm) * direction
                res_norm = new_norm
        return correction

    solved = jnp.zeros_like(residual)
    for turn in range(OUTER):
        correction = solve(residual)
        corrs[turn, row] = correction.astype(jnp.bfloat16)
        spread(*corr_args[turn])
        if turn == 0:
            arrive(*feat_args)
            for b in range(n_rows):
                tiles[:, b * block : (b + 1) * block] = tile_of(feats[b])
        arrive(*corr_args[turn])
        everyone = jnp.concatenate([corrs[turn, b] for b in range(n_rows)], axis=1)
        applied = noise_col * correction + lax.dot_general(
            everyone, tiles[...], (((1,), (1,)), ((), ())), preferred_element_type=jnp.float32
        )
        cross = jnp.sum(residual * applied, 1, keepdims=True)
        energy = jnp.sum(applied * applied, 1, keepdims=True)
        sums[turn, row] = to_row((cross, energy), sums.shape[-1])
        spread(*sum_args[turn])
        arrive(*sum_args[turn])
        total = jnp.sum(sums[turn], 0)
        damping = to_column(total, own_rhs) / (to_column(total, own_rhs, own_rhs) + 1e-06)
        solved = solved + damping * correction
        residual = residual - damping * applied

    def end_copy(k, slot):
        return pltpu.make_async_remote_copy(
            src_ref=ends.at[slot],
            dst_ref=ends.at[slot],
            send_sem=end_send.at[k],
            recv_sem=end_recv.at[k],
            device_id=(row, col_peer(k)),
            device_id_type=MESH,
        )

    ends[col, 0] = solved
    ends[col, 1] = residual
    each(n_cols, lambda k: end_copy(k, col).start())

    each(n_cols, lambda k: part_copy(k, col_peer(k), col).wait_send())
    for copy in (feat_args, *corr_args, *sum_args):
        each(n_rows, lambda k: row_copy(*copy, k, row).wait_send())

    def own_points(field):
        points = field[:, :own_len]
        for c in range(1, n_cols):
            points = jnp.where(col == c, field[:, c * own_len : (c + 1) * own_len], points)
        return points

    each(n_cols, lambda k: end_copy(k, col_peer(n_cols - k)).wait_recv())
    for c in range(n_cols):
        sol_ref[c * own_rhs : (c + 1) * own_rhs, :] = own_points(ends[c, 0])
        res_ref[c * own_rhs : (c + 1) * own_rhs, :] = own_points(ends[c, 1])
    each(n_cols, lambda k: end_copy(k, col).wait_send())


def body_small(n_rows, n_cols, features, targets, point_order, lengthscale, noise_var):
    n_feats, own_len = features.shape
    rhs = targets.shape[0]
    own_rhs = rhs // n_cols
    block = n_cols * own_len
    out = jax.ShapeDtypeStruct((rhs, own_len), jnp.float32)
    args = (features, targets, point_order[None, :], lengthscale[None, :], noise_var[None, :])
    dma = pltpu.SemaphoreType.DMA
    return pl.pallas_call(
        functools.partial(fused, n_rows, n_cols),
        out_shape=(out, out),
        in_specs=[pl.BlockSpec(memory_space=pl.ANY)] * len(args),
        out_specs=(pl.BlockSpec(memory_space=pltpu.VMEM),) * 2,
        scratch_shapes=[
            *(pltpu.VMEM(arg.shape, arg.dtype) for arg in args),
            pltpu.VMEM((n_cols, n_feats + own_rhs + 8, block), jnp.float32),
            pltpu.VMEM((n_cols, n_feats + own_rhs + 8, block), jnp.float32),
            pltpu.VMEM((n_rows, n_feats, block), jnp.float32),
            pltpu.VMEM((block, n_rows * block), jnp.bfloat16),
            pltpu.VMEM((OUTER, n_rows, own_rhs, block), jnp.bfloat16),
            pltpu.VMEM((OUTER, n_rows, 1, 128), jnp.float32),
            pltpu.VMEM((n_cols, 2, own_rhs, block), jnp.float32),
            dma((len(args),)),
            dma((n_cols,)),
            dma((n_cols,)),
            dma((n_rows,)),
            dma((n_rows,)),
            dma((OUTER, n_rows)),
            dma((OUTER, n_rows)),
            dma((OUTER, n_rows)),
            dma((OUTER, n_rows)),
            dma((n_cols,)),
            dma((n_cols,)),
        ],
        compiler_params=pltpu.CompilerParams(
            collective_id=0, has_side_effects=True, vmem_limit_bytes=32 * 1024 * 1024
        ),
    )(*args)


def body(n_rows, n_cols, features, targets, point_order, lengthscale, noise_var):
    n_feats, own_len = features.shape
    rhs = targets.shape[0]
    block = n_cols * own_len
    args = (features, targets, point_order, lengthscale, noise_var)
    fits = 2 * n_rows * block * block <= 8 * 1024 * 1024
    even = block % 128 == 0 and rhs % (16 * n_cols) == 0 and n_feats % 8 == 0
    even = even and 2 * rhs // n_cols <= 128
    if fits and even and n_rows > 1 and n_cols > 1:
        return body_small(n_rows, n_cols, *args)
    return body_large(*args)


def solution(mesh):
    return jax.shard_map(
        functools.partial(body, mesh.shape["rows"], mesh.shape["cols"]),
        mesh=mesh,
        in_specs=(
            P(None, ("rows", "cols")),
            P(None, ("rows", "cols")),
            P(("rows", "cols")),
            P(),
            P(),
        ),
        out_specs=(P(None, ("rows", "cols")), P(None, ("rows", "cols"))),
        check_vma=False,
    )
```

```python
import functools
import math

import jax
import jax.numpy as jnp
from jax import lax
from jax.experimental import pallas as pl
from jax.experimental.pallas import tpu as pltpu
from jax.sharding import PartitionSpec as P

INNER = 3
OUTER = 2
MESH = pl.DeviceIdType.MESH


def kernel_tile(col_feat, col_norm, row_feat, row_norm):
    inner_prod = jnp.dot(
        col_feat.T, row_feat, precision=lax.Precision.HIGHEST, preferred_element_type=jnp.float32
    )
    return jnp.exp(-0.5 * (col_norm[:, None] + row_norm[None, :] - 2.0 * inner_prod)).astype(
        jnp.bfloat16
    )


def apply_columns(running, portion, col_feat, col_norm, row_feat, row_norm):
    columns = portion.shape[1]
    sub_cols = math.gcd(columns, 512)

    def advance(which, summed):
        offset = which * sub_cols
        part_feat = lax.dynamic_slice_in_dim(col_feat, offset, sub_cols, 1)
        part_norm = lax.dynamic_slice_in_dim(col_norm, offset, sub_cols, 0)
        part_vec = lax.dynamic_slice_in_dim(portion, offset, sub_cols, 1)
        kern_tile = kernel_tile(part_feat, part_norm, row_feat, row_norm)
        return summed + jnp.dot(part_vec, kern_tile, preferred_element_type=jnp.float32)

    return lax.fori_loop(0, columns // sub_cols, advance, running)


def body_large(features, targets, point_order, lengthscale, noise_var):
    scaled = features / lengthscale[:, None]
    row_norms = jnp.sum(scaled * scaled, 0)
    block_feat, block_targ = (
        lax.all_gather(scaled, "cols", axis=1, tiled=True),
        lax.all_gather(targets, "cols", axis=1, tiled=True),
    )
    block_norms = jnp.sum(block_feat * block_feat, 0)
    block_first = lax.axis_index("rows") * block_feat.shape[1]
    residual = jnp.take(block_targ, point_order - block_first, axis=1)
    noise_col = noise_var[:, None]
    own_len = scaled.shape[1]
    col_feat = lax.all_gather(scaled, ("rows", "cols"), axis=1, tiled=True)
    col_norm = jnp.sum(col_feat * col_feat, 0)
    solution = jnp.zeros_like(residual)
    for outer_turn in range(OUTER):
        remains = lax.all_gather(residual, "cols", axis=1, tiled=True)
        res_norm = jnp.sum(remains * remains, 1)
        direction = remains
        correction = jnp.zeros_like(remains)
        for inner_turn in range(INNER):
            block_packed = direction.astype(jnp.bfloat16)
            blank_block = jnp.zeros(block_packed.shape, jnp.float32)
            applied = (
                apply_columns(
                    blank_block, block_packed, block_feat, block_norms, block_feat, block_norms
                )
                + noise_col * direction
            )
            curvature = jnp.sum(direction * applied, 1)
            step_len = res_norm / curvature
            correction = correction + step_len[:, None] * direction
            remains = remains - step_len[:, None] * applied
            if inner_turn + 1 < INNER:
                new_norm = jnp.sum(remains * remains, 1)
                direction = remains + (new_norm / res_norm)[:, None] * direction
                res_norm = new_norm
        correction = lax.dynamic_slice_in_dim(
            correction, lax.axis_index("cols") * own_len, own_len, 1
        )
        packed = correction.astype(jnp.bfloat16)
        blank = jnp.zeros((packed.shape[0], scaled.shape[1]), jnp.float32)
        applied = (
            apply_columns(
                blank,
                lax.all_gather(packed, ("rows", "cols"), axis=1, tiled=True),
                col_feat,
                col_norm,
                scaled,
                row_norms,
            )
            + noise_col * correction
        )
        cross_term, energy = lax.psum(
            (jnp.sum(residual * applied, 1), jnp.sum(applied * applied, 1)), ("rows", "cols")
        )
        damping_w = cross_term / (energy + 1e-06)
        solution = solution + damping_w[:, None] * correction
        residual = residual - damping_w[:, None] * applied
    return (solution, residual)


def to_column(row, rows, first=0):
    shape = (rows, row.shape[1])
    at, lane = (lax.broadcasted_iota(jnp.int32, shape, axis) for axis in (0, 1))
    return jnp.sum(jnp.where(at + first == lane, row, 0.0), 1, keepdims=True)


def three_parts(x):
    high = x.astype(jnp.bfloat16).astype(jnp.float32)
    mid = (x - high).astype(jnp.bfloat16).astype(jnp.float32)
    low = ((x - high) - mid).astype(jnp.bfloat16).astype(jnp.float32)
    return high, mid, low


def fused(
    n_rows,
    n_cols,
    feat_hbm,
    targ_hbm,
    order_hbm,
    length_hbm,
    noise_hbm,
    sol_ref,
    res_ref,
    feat_ref,
    targ_ref,
    order_ref,
    length_ref,
    noise_ref,
    parts_out,
    parts,
    feats,
    stacks,
    tiles,
    fields,
    ends,
    load_sem,
    part_send,
    part_recv,
    feat_send,
    feat_recv,
    end_send,
    end_recv,
):
    row, col = lax.axis_index("rows"), lax.axis_index("cols")
    n_feats, own_len = feat_ref.shape
    own_rhs = targ_ref.shape[0] // n_cols
    block = n_cols * own_len

    def row_peer(k):
        return lax.rem(row + k, n_rows)

    def col_peer(k):
        return lax.rem(col + k, n_cols)

    def each(count, step):
        def one(k, carry):
            step(k)
            return carry

        lax.fori_loop(1, count, one, 0)

    loads = [
        pltpu.make_async_copy(source, target, load_sem.at[which])
        for which, (source, target) in enumerate(
            (
                (feat_hbm, feat_ref),
                (targ_hbm, targ_ref),
                (order_hbm, order_ref),
                (length_hbm, length_ref),
                (noise_hbm, noise_ref),
            )
        )
    ]
    for load in loads:
        load.start()

    barrier = pltpu.get_barrier_semaphore()
    each(
        n_cols,
        lambda k: pl.semaphore_signal(
            barrier, inc=1, device_id=(row, col_peer(k)), device_id_type=MESH
        ),
    )
    each(
        n_rows,
        lambda k: pl.semaphore_signal(
            barrier, inc=1, device_id=(row_peer(k), col), device_id_type=MESH
        ),
    )
    for load in loads:
        load.wait()

    noise_col = to_column(noise_ref[...], own_rhs, col * own_rhs)
    scaled = feat_ref[...] / to_column(length_ref[...], n_feats)
    order = (order_ref[...] - row * block).astype(jnp.float32)
    order = jnp.broadcast_to(order, (8, own_len))
    for c in range(n_cols):
        share = targ_ref[c * own_rhs : (c + 1) * own_rhs, :]
        own = jnp.concatenate([scaled, share, order], axis=0)
        wide = jnp.concatenate([own] * n_cols, axis=1)
        lane = lax.broadcasted_iota(jnp.int32, wide.shape, 1)
        parts_out[c] = jnp.where(lane // own_len == col, wide, 0.0)
    pl.semaphore_wait(barrier, n_rows - 1 + n_cols - 1)

    def part_copy(k, target, slot):
        return pltpu.make_async_remote_copy(
            src_ref=parts_out.at[target],
            dst_ref=parts.at[slot],
            send_sem=part_send.at[k],
            recv_sem=part_recv.at[k],
            device_id=(row, target),
            device_id_type=MESH,
        )

    each(n_cols, lambda k: part_copy(k, col_peer(k), col).start())
    parts[col] = parts_out[col]
    each(n_cols, lambda k: part_copy(k, col_peer(k), col_peer(n_cols - k)).wait_recv())
    whole = parts[0]
    for c in range(1, n_cols):
        whole = whole + parts[c]
    block_feat = whole[:n_feats]
    block_targ = whole[n_feats : n_feats + own_rhs]
    block_order = whole[n_feats + own_rhs : n_feats + own_rhs + 1]
    def row_copy(buffer, send_sem, recv_sem, k, slot):
        return pltpu.make_async_remote_copy(
            src_ref=buffer.at[slot],
            dst_ref=buffer.at[slot],
            send_sem=send_sem.at[k],
            recv_sem=recv_sem.at[k],
            device_id=(row_peer(k), col),
            device_id_type=MESH,
        )

    def spread(*copy):
        each(n_rows, lambda k: row_copy(*copy, k, row).start())

    def arrive(*copy):
        each(n_rows, lambda k: row_copy(*copy, k, row_peer(n_rows - k)).wait_recv())

    place = lax.broadcasted_iota(jnp.int32, (block, block), 0).astype(jnp.float32)
    picked = jnp.where(place == block_order, 1.0, 0.0).astype(jnp.bfloat16)
    three = jnp.concatenate(three_parts(block_targ), axis=0).astype(jnp.bfloat16)
    three = jnp.dot(three, picked, preferred_element_type=jnp.float32)
    residual = (three[:own_rhs] + three[own_rhs : 2 * own_rhs]) + three[2 * own_rhs :]

    everything = (feats, feat_send, feat_recv)
    feats[row] = jnp.concatenate([block_feat, residual], axis=0)
    spread(*everything)
    arrive(*everything)

    spare = lax.broadcasted_iota(jnp.int32, (16, block), 0)
    log2e = 1.4426950408889634

    def stack_of(feat, left):
        high, mid, low = three_parts(feat * log2e if left else feat)
        norm = three_parts((-0.5 * log2e) * jnp.sum(feat * feat, 0, keepdims=True))
        first = 0 if left else 3
        tail = jnp.where(spare < 6, 1.0, 0.0)
        for which, part in enumerate(norm):
            tail = jnp.where(spare == first + which, part, tail)
        if left:
            return jnp.concatenate([high, high, mid, mid, high, low, tail], axis=0)
        return jnp.concatenate([high, mid, high, mid, low, high, tail], axis=0)

    right = jnp.concatenate(
        [stack_of(feats[b, :n_feats, :], False).astype(jnp.bfloat16) for b in range(n_rows)], axis=1
    )
    stacks[...] = right
    points = n_rows * block
    span = math.gcd(points, 4 * block)

    def fill(b, carry):
        left = jnp.transpose(stack_of(feats[b, :n_feats, :], True)).astype(jnp.bfloat16)
        rows = pl.ds(pl.multiple_of(b * block, block), block)
        for first in range(0, points, span):
            power = jnp.dot(
                left, stacks[:, first : first + span], preferred_element_type=jnp.float32
            )
            tiles[rows, first : first + span] = jnp.exp2(power).astype(jnp.bfloat16)
        return carry

    lax.fori_loop(0, n_rows, fill, 0)

    noise_all = jnp.concatenate([noise_col] * n_rows, axis=0)

    def block_images(packed):
        return jnp.concatenate(
            [
                jnp.dot(
                    packed[b * own_rhs : (b + 1) * own_rhs],
                    tiles[b * block : (b + 1) * block, b * block : (b + 1) * block],
                    preferred_element_type=jnp.float32,
                )
                for b in range(n_rows)
            ],
            axis=0,
        )

    def over_blocks(field):
        summed = field[:own_rhs]
        for b in range(1, n_rows):
            summed = summed + field[b * own_rhs : (b + 1) * own_rhs]
        return jnp.sum(summed, 1, keepdims=True)

    def solve(residual):
        remains = residual
        res_norm = jnp.sum(remains * remains, 1, keepdims=True)
        direction = remains
        correction = jnp.zeros_like(remains)
        for inner_turn in range(INNER):
            image = block_images(direction.astype(jnp.bfloat16)) + noise_all * direction
            step_len = res_norm / jnp.sum(direction * image, 1, keepdims=True)
            correction = correction + step_len * direction
            if inner_turn + 1 < INNER:
                remains = remains - step_len * image
                new_norm = jnp.sum(remains * remains, 1, keepdims=True)
                direction = remains + (new_norm / res_norm) * direction
                res_norm = new_norm
        return correction

    residual = jnp.concatenate([feats[b, n_feats:, :] for b in range(n_rows)], axis=0)
    solved = jnp.zeros_like(residual)
    for turn in range(OUTER):
        correction = solve(residual)
        packed = correction.astype(jnp.bfloat16)
        packed = jnp.concatenate(
            [packed[b * own_rhs : (b + 1) * own_rhs] for b in range(n_rows)], axis=1
        )
        full = jnp.dot(packed, tiles[...], preferred_element_type=jnp.float32)
        applied = noise_all * correction + jnp.concatenate(
            [full[:, b * block : (b + 1) * block] for b in range(n_rows)], axis=0
        )
        damping = over_blocks(residual * applied) / (over_blocks(applied * applied) + 1e-06)
        damping = jnp.concatenate([damping] * n_rows, axis=0)
        solved = solved + damping * correction
        residual = residual - damping * applied
    fields[0] = solved
    fields[1] = residual
    own_rows = pl.ds(pl.multiple_of(row * own_rhs, own_rhs), own_rhs)
    solved = fields[0, own_rows, :]
    residual = fields[1, own_rows, :]

    def end_copy(k, slot):
        return pltpu.make_async_remote_copy(
            src_ref=ends.at[slot],
            dst_ref=ends.at[slot],
            send_sem=end_send.at[k],
            recv_sem=end_recv.at[k],
            device_id=(row, col_peer(k)),
            device_id_type=MESH,
        )

    ends[col, 0] = solved
    ends[col, 1] = residual
    each(n_cols, lambda k: end_copy(k, col).start())

    each(n_cols, lambda k: part_copy(k, col_peer(k), col).wait_send())
    each(n_rows, lambda k: row_copy(*everything, k, row).wait_send())

    def own_points(field):
        points = field[:, :own_len]
        for c in range(1, n_cols):
            points = jnp.where(col == c, field[:, c * own_len : (c + 1) * own_len], points)
        return points

    each(n_cols, lambda k: end_copy(k, col_peer(n_cols - k)).wait_recv())
    for c in range(n_cols):
        sol_ref[c * own_rhs : (c + 1) * own_rhs, :] = own_points(ends[c, 0])
        res_ref[c * own_rhs : (c + 1) * own_rhs, :] = own_points(ends[c, 1])
    each(n_cols, lambda k: end_copy(k, col).wait_send())


def body_small(n_rows, n_cols, features, targets, point_order, lengthscale, noise_var):
    n_feats, own_len = features.shape
    rhs = targets.shape[0]
    own_rhs = rhs // n_cols
    block = n_cols * own_len
    out = jax.ShapeDtypeStruct((rhs, own_len), jnp.float32)
    args = (features, targets, point_order[None, :], lengthscale[None, :], noise_var[None, :])
    dma = pltpu.SemaphoreType.DMA
    return pl.pallas_call(
        functools.partial(fused, n_rows, n_cols),
        out_shape=(out, out),
        in_specs=[pl.BlockSpec(memory_space=pl.ANY)] * len(args),
        out_specs=(pl.BlockSpec(memory_space=pltpu.VMEM),) * 2,
        scratch_shapes=[
            *(pltpu.VMEM(arg.shape, arg.dtype) for arg in args),
            pltpu.VMEM((n_cols, n_feats + own_rhs + 8, block), jnp.float32),
            pltpu.VMEM((n_cols, n_feats + own_rhs + 8, block), jnp.float32),
            pltpu.VMEM((n_rows, n_feats + own_rhs, block), jnp.float32),
            pltpu.VMEM((6 * n_feats + 16, n_rows * block), jnp.bfloat16),
            pltpu.VMEM((n_rows * block, n_rows * block), jnp.bfloat16),
            pltpu.VMEM((2, n_rows * own_rhs, block), jnp.float32),
            pltpu.VMEM((n_cols, 2, own_rhs, block), jnp.float32),
            dma((len(args),)),
            dma((n_cols,)),
            dma((n_cols,)),
            dma((n_rows,)),
            dma((n_rows,)),
            dma((n_cols,)),
            dma((n_cols,)),
        ],
        compiler_params=pltpu.CompilerParams(
            collective_id=0, has_side_effects=True, vmem_limit_bytes=48 * 1024 * 1024
        ),
    )(*args)


def body(n_rows, n_cols, features, targets, point_order, lengthscale, noise_var):
    n_feats, own_len = features.shape
    rhs = targets.shape[0]
    block = n_cols * own_len
    args = (features, targets, point_order, lengthscale, noise_var)
    fits = 2 * (n_rows * block) ** 2 <= 16 * 1024 * 1024
    even = block % 128 == 0 and rhs % (16 * n_cols) == 0 and n_feats % 16 == 0
    if fits and even and n_rows > 1 and n_cols > 1:
        return body_small(n_rows, n_cols, *args)
    return body_large(*args)


def solution(mesh):
    return jax.shard_map(
        functools.partial(body, mesh.shape["rows"], mesh.shape["cols"]),
        mesh=mesh,
        in_specs=(
            P(None, ("rows", "cols")),
            P(None, ("rows", "cols")),
            P(("rows", "cols")),
            P(),
            P(),
        ),
        out_specs=(P(None, ("rows", "cols")), P(None, ("rows", "cols"))),
        check_vma=False,
    )
```

```python
import functools
import math

import jax
import jax.numpy as jnp
from jax import lax
from jax.experimental import pallas as pl
from jax.experimental.pallas import tpu as pltpu
from jax.sharding import PartitionSpec as P

INNER = 3
OUTER = 2
MESH = pl.DeviceIdType.MESH


def kernel_tile(col_feat, col_norm, row_feat, row_norm):
    inner_prod = jnp.dot(
        col_feat.T, row_feat, precision=lax.Precision.HIGHEST, preferred_element_type=jnp.float32
    )
    return jnp.exp(-0.5 * (col_norm[:, None] + row_norm[None, :] - 2.0 * inner_prod)).astype(
        jnp.bfloat16
    )


def apply_columns(running, portion, col_feat, col_norm, row_feat, row_norm):
    columns = portion.shape[1]
    sub_cols = math.gcd(columns, 512)

    def advance(which, summed):
        offset = which * sub_cols
        part_feat = lax.dynamic_slice_in_dim(col_feat, offset, sub_cols, 1)
        part_norm = lax.dynamic_slice_in_dim(col_norm, offset, sub_cols, 0)
        part_vec = lax.dynamic_slice_in_dim(portion, offset, sub_cols, 1)
        kern_tile = kernel_tile(part_feat, part_norm, row_feat, row_norm)
        return summed + jnp.dot(part_vec, kern_tile, preferred_element_type=jnp.float32)

    return lax.fori_loop(0, columns // sub_cols, advance, running)


def body_large(features, targets, point_order, lengthscale, noise_var):
    scaled = features / lengthscale[:, None]
    row_norms = jnp.sum(scaled * scaled, 0)
    block_feat, block_targ = (
        lax.all_gather(scaled, "cols", axis=1, tiled=True),
        lax.all_gather(targets, "cols", axis=1, tiled=True),
    )
    block_norms = jnp.sum(block_feat * block_feat, 0)
    block_first = lax.axis_index("rows") * block_feat.shape[1]
    residual = jnp.take(block_targ, point_order - block_first, axis=1)
    noise_col = noise_var[:, None]
    own_len = scaled.shape[1]
    col_feat = lax.all_gather(scaled, ("rows", "cols"), axis=1, tiled=True)
    col_norm = jnp.sum(col_feat * col_feat, 0)
    solution = jnp.zeros_like(residual)
    for outer_turn in range(OUTER):
        remains = lax.all_gather(residual, "cols", axis=1, tiled=True)
        res_norm = jnp.sum(remains * remains, 1)
        direction = remains
        correction = jnp.zeros_like(remains)
        for inner_turn in range(INNER):
            block_packed = direction.astype(jnp.bfloat16)
            blank_block = jnp.zeros(block_packed.shape, jnp.float32)
            applied = (
                apply_columns(
                    blank_block, block_packed, block_feat, block_norms, block_feat, block_norms
                )
                + noise_col * direction
            )
            curvature = jnp.sum(direction * applied, 1)
            step_len = res_norm / curvature
            correction = correction + step_len[:, None] * direction
            remains = remains - step_len[:, None] * applied
            if inner_turn + 1 < INNER:
                new_norm = jnp.sum(remains * remains, 1)
                direction = remains + (new_norm / res_norm)[:, None] * direction
                res_norm = new_norm
        correction = lax.dynamic_slice_in_dim(
            correction, lax.axis_index("cols") * own_len, own_len, 1
        )
        packed = correction.astype(jnp.bfloat16)
        blank = jnp.zeros((packed.shape[0], scaled.shape[1]), jnp.float32)
        applied = (
            apply_columns(
                blank,
                lax.all_gather(packed, ("rows", "cols"), axis=1, tiled=True),
                col_feat,
                col_norm,
                scaled,
                row_norms,
            )
            + noise_col * correction
        )
        cross_term, energy = lax.psum(
            (jnp.sum(residual * applied, 1), jnp.sum(applied * applied, 1)), ("rows", "cols")
        )
        damping_w = cross_term / (energy + 1e-06)
        solution = solution + damping_w[:, None] * correction
        residual = residual - damping_w[:, None] * applied
    return (solution, residual)


def to_column(row, rows, first=0):
    shape = (rows, row.shape[1])
    at, lane = (lax.broadcasted_iota(jnp.int32, shape, axis) for axis in (0, 1))
    return jnp.sum(jnp.where(at + first == lane, row, 0.0), 1, keepdims=True)


def three_parts(x):
    high = x.astype(jnp.bfloat16).astype(jnp.float32)
    mid = (x - high).astype(jnp.bfloat16).astype(jnp.float32)
    low = ((x - high) - mid).astype(jnp.bfloat16).astype(jnp.float32)
    return high, mid, low


def fused(
    n_rows,
    n_cols,
    feat_hbm,
    targ_hbm,
    order_hbm,
    length_hbm,
    noise_hbm,
    sol_ref,
    res_ref,
    feat_ref,
    targ_ref,
    order_ref,
    length_ref,
    noise_ref,
    parts_out,
    parts,
    feats,
    resids,
    stacks,
    tiles,
    fields,
    ends,
    load_sem,
    part_send,
    part_recv,
    feat_send,
    feat_recv,
    resid_send,
    resid_recv,
    end_send,
    end_recv,
):
    row, col = lax.axis_index("rows"), lax.axis_index("cols")
    n_feats, own_len = feat_ref.shape
    own_rhs = targ_ref.shape[0] // n_cols
    block = n_cols * own_len

    def row_peer(k):
        return lax.rem(row + k, n_rows)

    def col_peer(k):
        return lax.rem(col + k, n_cols)

    def each(count, step):
        def one(k, carry):
            step(k)
            return carry

        lax.fori_loop(1, count, one, 0)

    loads = [
        pltpu.make_async_copy(source, target, load_sem.at[which])
        for which, (source, target) in enumerate(
            (
                (feat_hbm, feat_ref),
                (targ_hbm, targ_ref),
                (order_hbm, order_ref),
                (length_hbm, length_ref),
                (noise_hbm, noise_ref),
            )
        )
    ]
    for load in loads:
        load.start()

    barrier = pltpu.get_barrier_semaphore()
    each(
        n_cols,
        lambda k: pl.semaphore_signal(
            barrier, inc=1, device_id=(row, col_peer(k)), device_id_type=MESH
        ),
    )
    each(
        n_rows,
        lambda k: pl.semaphore_signal(
            barrier, inc=1, device_id=(row_peer(k), col), device_id_type=MESH
        ),
    )
    for load in loads:
        load.wait()

    noise_col = to_column(noise_ref[...], own_rhs, col * own_rhs)
    scaled = feat_ref[...] / to_column(length_ref[...], n_feats)
    order = (order_ref[...] - row * block).astype(jnp.float32)
    order = jnp.broadcast_to(order, (8, own_len))
    for c in range(n_cols):
        share = targ_ref[c * own_rhs : (c + 1) * own_rhs, :]
        own = jnp.concatenate([scaled, share, order], axis=0)
        wide = jnp.concatenate([own] * n_cols, axis=1)
        lane = lax.broadcasted_iota(jnp.int32, wide.shape, 1)
        parts_out[c] = jnp.where(lane // own_len == col, wide, 0.0)
    pl.semaphore_wait(barrier, n_rows - 1 + n_cols - 1)

    def part_copy(k, target, slot):
        return pltpu.make_async_remote_copy(
            src_ref=parts_out.at[target],
            dst_ref=parts.at[slot],
            send_sem=part_send.at[k],
            recv_sem=part_recv.at[k],
            device_id=(row, target),
            device_id_type=MESH,
        )

    each(n_cols, lambda k: part_copy(k, col_peer(k), col).start())
    parts[col] = parts_out[col]
    each(n_cols, lambda k: part_copy(k, col_peer(k), col_peer(n_cols - k)).wait_recv())
    whole = parts[0]
    for c in range(1, n_cols):
        whole = whole + parts[c]
    block_feat = whole[:n_feats]
    block_targ = whole[n_feats : n_feats + own_rhs]
    block_order = whole[n_feats + own_rhs : n_feats + own_rhs + 1]
    def row_copy(buffer, send_sem, recv_sem, k, slot):
        return pltpu.make_async_remote_copy(
            src_ref=buffer.at[slot],
            dst_ref=buffer.at[slot],
            send_sem=send_sem.at[k],
            recv_sem=recv_sem.at[k],
            device_id=(row_peer(k), col),
            device_id_type=MESH,
        )

    def spread(*copy):
        each(n_rows, lambda k: row_copy(*copy, k, row).start())

    def arrive(*copy):
        each(n_rows, lambda k: row_copy(*copy, k, row_peer(n_rows - k)).wait_recv())

    feat_args = (feats, feat_send, feat_recv)
    feats[row] = block_feat
    spread(*feat_args)

    place = lax.broadcasted_iota(jnp.int32, (block, block), 0).astype(jnp.float32)
    picked = jnp.where(place == block_order, 1.0, 0.0).astype(jnp.bfloat16)
    three = jnp.concatenate(three_parts(block_targ), axis=0).astype(jnp.bfloat16)
    three = jnp.dot(three, picked, preferred_element_type=jnp.float32)
    residual = (three[:own_rhs] + three[own_rhs : 2 * own_rhs]) + three[2 * own_rhs :]

    resid_args = (resids, resid_send, resid_recv)
    resids[row] = residual
    spread(*resid_args)
    arrive(*feat_args)

    spare = lax.broadcasted_iota(jnp.int32, (16, block), 0)
    log2e = 1.4426950408889634

    def stack_of(feat, left):
        high, mid, low = three_parts(feat * log2e if left else feat)
        norm = three_parts((-0.5 * log2e) * jnp.sum(feat * feat, 0, keepdims=True))
        first = 0 if left else 3
        tail = jnp.where(spare < 6, 1.0, 0.0)
        for which, part in enumerate(norm):
            tail = jnp.where(spare == first + which, part, tail)
        if left:
            return jnp.concatenate([high, high, mid, mid, high, low, tail], axis=0)
        return jnp.concatenate([high, mid, high, mid, low, high, tail], axis=0)

    right = jnp.concatenate(
        [stack_of(feats[b], False).astype(jnp.bfloat16) for b in range(n_rows)], axis=1
    )
    stacks[...] = right
    points = n_rows * block
    span = math.gcd(points, 4 * block)

    def fill(b, carry):
        left = jnp.transpose(stack_of(feats[b], True)).astype(jnp.bfloat16)
        rows = pl.ds(pl.multiple_of(b * block, block), block)
        for first in range(0, points, span):
            power = jnp.dot(
                left, stacks[:, first : first + span], preferred_element_type=jnp.float32
            )
            tiles[rows, first : first + span] = jnp.exp2(power).astype(jnp.bfloat16)
        return carry

    lax.fori_loop(0, n_rows, fill, 0)

    noise_all = jnp.concatenate([noise_col] * n_rows, axis=0)

    def block_images(packed):
        return jnp.concatenate(
            [
                jnp.dot(
                    packed[b * own_rhs : (b + 1) * own_rhs],
                    tiles[b * block : (b + 1) * block, b * block : (b + 1) * block],
                    preferred_element_type=jnp.float32,
                )
                for b in range(n_rows)
            ],
            axis=0,
        )

    def over_blocks(field):
        summed = field[:own_rhs]
        for b in range(1, n_rows):
            summed = summed + field[b * own_rhs : (b + 1) * own_rhs]
        return jnp.sum(summed, 1, keepdims=True)

    def solve(residual):
        remains = residual
        res_norm = jnp.sum(remains * remains, 1, keepdims=True)
        direction = remains
        correction = jnp.zeros_like(remains)
        for inner_turn in range(INNER):
            image = block_images(direction.astype(jnp.bfloat16)) + noise_all * direction
            step_len = res_norm / jnp.sum(direction * image, 1, keepdims=True)
            correction = correction + step_len * direction
            if inner_turn + 1 < INNER:
                remains = remains - step_len * image
                new_norm = jnp.sum(remains * remains, 1, keepdims=True)
                direction = remains + (new_norm / res_norm) * direction
                res_norm = new_norm
        return correction

    arrive(*resid_args)
    residual = jnp.concatenate([resids[b] for b in range(n_rows)], axis=0)
    solved = jnp.zeros_like(residual)
    for turn in range(OUTER):
        correction = solve(residual)
        packed = correction.astype(jnp.bfloat16)
        packed = jnp.concatenate(
            [packed[b * own_rhs : (b + 1) * own_rhs] for b in range(n_rows)], axis=1
        )
        full = jnp.dot(packed, tiles[...], preferred_element_type=jnp.float32)
        applied = noise_all * correction + jnp.concatenate(
            [full[:, b * block : (b + 1) * block] for b in range(n_rows)], axis=0
        )
        damping = over_blocks(residual * applied) / (over_blocks(applied * applied) + 1e-06)
        damping = jnp.concatenate([damping] * n_rows, axis=0)
        solved = solved + damping * correction
        residual = residual - damping * applied
    fields[0] = solved
    fields[1] = residual
    own_rows = pl.ds(pl.multiple_of(row * own_rhs, own_rhs), own_rhs)
    solved = fields[0, own_rows, :]
    residual = fields[1, own_rows, :]

    def end_copy(k, slot):
        return pltpu.make_async_remote_copy(
            src_ref=ends.at[slot],
            dst_ref=ends.at[slot],
            send_sem=end_send.at[k],
            recv_sem=end_recv.at[k],
            device_id=(row, col_peer(k)),
            device_id_type=MESH,
        )

    ends[col, 0] = solved
    ends[col, 1] = residual
    each(n_cols, lambda k: end_copy(k, col).start())

    each(n_cols, lambda k: part_copy(k, col_peer(k), col).wait_send())
    for copy in (feat_args, resid_args):
        each(n_rows, lambda k: row_copy(*copy, k, row).wait_send())

    def own_points(field):
        points = field[:, :own_len]
        for c in range(1, n_cols):
            points = jnp.where(col == c, field[:, c * own_len : (c + 1) * own_len], points)
        return points

    each(n_cols, lambda k: end_copy(k, col_peer(n_cols - k)).wait_recv())
    for c in range(n_cols):
        sol_ref[c * own_rhs : (c + 1) * own_rhs, :] = own_points(ends[c, 0])
        res_ref[c * own_rhs : (c + 1) * own_rhs, :] = own_points(ends[c, 1])
    each(n_cols, lambda k: end_copy(k, col).wait_send())


def body_small(n_rows, n_cols, features, targets, point_order, lengthscale, noise_var):
    n_feats, own_len = features.shape
    rhs = targets.shape[0]
    own_rhs = rhs // n_cols
    block = n_cols * own_len
    out = jax.ShapeDtypeStruct((rhs, own_len), jnp.float32)
    args = (features, targets, point_order[None, :], lengthscale[None, :], noise_var[None, :])
    dma = pltpu.SemaphoreType.DMA
    return pl.pallas_call(
        functools.partial(fused, n_rows, n_cols),
        out_shape=(out, out),
        in_specs=[pl.BlockSpec(memory_space=pl.ANY)] * len(args),
        out_specs=(pl.BlockSpec(memory_space=pltpu.VMEM),) * 2,
        scratch_shapes=[
            *(pltpu.VMEM(arg.shape, arg.dtype) for arg in args),
            pltpu.VMEM((n_cols, n_feats + own_rhs + 8, block), jnp.float32),
            pltpu.VMEM((n_cols, n_feats + own_rhs + 8, block), jnp.float32),
            pltpu.VMEM((n_rows, n_feats, block), jnp.float32),
            pltpu.VMEM((n_rows, own_rhs, block), jnp.float32),
            pltpu.VMEM((6 * n_feats + 16, n_rows * block), jnp.bfloat16),
            pltpu.VMEM((n_rows * block, n_rows * block), jnp.bfloat16),
            pltpu.VMEM((2, n_rows * own_rhs, block), jnp.float32),
            pltpu.VMEM((n_cols, 2, own_rhs, block), jnp.float32),
            dma((len(args),)),
            dma((n_cols,)),
            dma((n_cols,)),
            dma((n_rows,)),
            dma((n_rows,)),
            dma((n_rows,)),
            dma((n_rows,)),
            dma((n_cols,)),
            dma((n_cols,)),
        ],
        compiler_params=pltpu.CompilerParams(
            collective_id=0, has_side_effects=True, vmem_limit_bytes=48 * 1024 * 1024
        ),
    )(*args)


def body(n_rows, n_cols, features, targets, point_order, lengthscale, noise_var):
    n_feats, own_len = features.shape
    rhs = targets.shape[0]
    block = n_cols * own_len
    args = (features, targets, point_order, lengthscale, noise_var)
    fits = 2 * (n_rows * block) ** 2 <= 16 * 1024 * 1024
    even = block % 128 == 0 and rhs % (16 * n_cols) == 0 and n_feats % 16 == 0
    if fits and even and n_rows > 1 and n_cols > 1:
        return body_small(n_rows, n_cols, *args)
    return body_large(*args)


def solution(mesh):
    return jax.shard_map(
        functools.partial(body, mesh.shape["rows"], mesh.shape["cols"]),
        mesh=mesh,
        in_specs=(
            P(None, ("rows", "cols")),
            P(None, ("rows", "cols")),
            P(("rows", "cols")),
            P(),
            P(),
        ),
        out_specs=(P(None, ("rows", "cols")), P(None, ("rows", "cols"))),
        check_vma=False,
    )
```
